256 devices in a mesh: space: 8 (over y, x_hi), group: 32 (over z, x_lo, core).
Axes of the slice: x: 4 (x_hi: 2, x_lo: 2; x = x_hi * 2 + x_lo), y: 4, z: 8, core: 2. Of those that a mesh axis runs over, the one named last changes fastest.
Arguments:
- perturbations: float32 [32, 4, 32, 64, 256], P('group', None, 'space'), may hold values from -6 to 6
- trajectory: bfloat16 [32, 8, 32, 64, 256], P('group', None, 'space'), may hold values from -0.25 to 0.25
- slot_table: int32 [32], replicated, may hold values from 0 to 31, each once
- step_indices: int32 [2], replicated, may hold values from 0 to 31
Outputs:
- evolved: float32 [32, 4, 32, 64, 256], P('group', None, 'space')
The draws below stay inside these ranges and needn't reach their ends.
Inputs may be any that keep to these rules, and one draw needn't show every extreme that they name: `slot_table`: each storage row appears exactly once.
All inputs are finite; a program needn't handle non-finite values.
Results may differ from the reference program's by a relative error of at most 0.00089.
Values may be sent and summed in bfloat16 or wider, within the bound.
No kernel may reach another device: no remote copies, remote signals or barrier semaphores. Data moves between devices by JAX's collectives and lax.ppermute only.
A program may use at most 64 MiB of HBM per device.

```python
import jax
import jax.numpy as jnp
from jax import lax

NZ = 64
NY = 256
STEPS = 2
PERTS = 32
NX = 32
SLICES = 32


def level_of(stream_key, shape, cuts, smallest, high):
    def one(dim, blocks):
        draws = jax.random.uniform(jax.random.fold_in(jax.random.fold_in(stream_key, 6), dim), (blocks,), jnp.float32, smallest / len(cuts), high / len(cuts))
        return jnp.repeat(jnp.exp(draws), shape[dim] // blocks).reshape((-1,) + (1,) * (len(shape) - dim - 1))

    loudness = one(*cuts[0])
    for cut in cuts[1:]:
        loudness = loudness * one(*cut)
    return loudness


def centred(rng, extent, width, limit, split=(), kind=jnp.bfloat16):
    result = width * jax.random.normal(rng, extent, jnp.float32)
    if split:
        result = result * level_of(rng, extent, split, -0.22, 0.18)
    return jnp.clip(result, -limit, limit).astype(kind)


def setup_inputs(seed: int = 0) -> dict:
    key_list = jax.random.split(jax.random.key(seed), 5)
    perturbations = centred(key_list[0], (PERTS, 4, NX, NZ, NY), 1.0, 6.0, ((0, 32), (2, 8)), jnp.float32)
    trajectory = jnp.clip(jax.random.uniform(key_list[1], (SLICES, 8, NX, NZ, NY), jnp.float32, -0.25, 0.25) * level_of(key_list[1], (SLICES, 8, NX, NZ, NY), ((0, 32), (2, 8)), -0.4, 0.0), -0.25, 0.25).astype(jnp.bfloat16)
    slot_table = jax.random.permutation(key_list[2], SLICES).astype(jnp.int32)
    step_indices = jax.random.randint(key_list[3], (STEPS,), 0, SLICES).astype(jnp.int32)
    return dict(perturbations=perturbations, trajectory=trajectory, slot_table=slot_table, step_indices=step_indices)


SATURATION_SLOPE = 2.0
SHARPNESS = 4.0
CONDENSE_RATE = 0.25
LATENT_HEAT = 0.3


def decode_slice(stored):
    decoded = stored.astype(jnp.float32)
    potential = 1.0 + 0.4 * decoded[4]
    exner_value = 1.0 + 0.4 * decoded[5]
    moisture = 1.0 + 2.0 * decoded[6]
    density = 1.0 + 0.8 * decoded[7]
    saturated = jnp.exp(SATURATION_SLOPE * (potential * exner_value - 1.0)) / density
    weight = jax.nn.sigmoid(SHARPNESS * (moisture - saturated))
    uptake = weight.astype(jnp.bfloat16)
    coupling = (weight * SATURATION_SLOPE * exner_value * saturated).astype(jnp.bfloat16)
    return lax.optimization_barrier(jnp.concatenate([stored[0:4], uptake[None], coupling[None]], axis=0))


def neighbour(source, position, upper_side):
    length = source.shape[position]
    zero_plane = jnp.zeros_like(lax.slice_in_dim(source, 0, 1, axis=position))
    if upper_side:
        return jnp.concatenate([lax.slice_in_dim(source, 1, length, axis=position), zero_plane], axis=position)
    return jnp.concatenate([zero_plane, lax.slice_in_dim(source, 0, length - 1, axis=position)], axis=position)


def upwind(velocity, centre, before, beyond):
    return jnp.maximum(velocity, 0.0) * (centre - before) + jnp.minimum(velocity, 0.0) * (beyond - centre)


def advance(fields, extended, coefficients):
    speeds = coefficients.astype(jnp.float32)
    east_cell = extended[:, 2:]
    west_cell = extended[:, :-2]
    south_cell = neighbour(fields, 3, False)
    north_cell = neighbour(fields, 3, True)
    below = neighbour(fields, 2, False)
    above = neighbour(fields, 2, True)
    diffusion = 0.025 + 0.06 * speeds[3]
    transport = upwind(speeds[0], fields, west_cell, east_cell)
    transport = transport + upwind(speeds[1], fields, south_cell, north_cell)
    transport = transport + upwind(speeds[2], fields, below, above)
    neighbours = east_cell + west_cell + north_cell + south_cell + above + below
    carried = fields - transport + diffusion * (neighbours - 6.0 * fields)
    condense = CONDENSE_RATE * (speeds[4] * carried[1] - speeds[5] * carried[0])
    return jnp.stack([carried[0] + LATENT_HEAT * condense, carried[1] - condense, carried[2] + condense, carried[3]])


def reference(perturbations, trajectory, slot_table, step_indices):
    current = perturbations
    for section in range(STEPS):
        storage_row = slot_table[step_indices[section]].astype(jnp.int32)
        stored = lax.dynamic_index_in_dim(trajectory, storage_row, 0, keepdims=False)
        coefficients = decode_slice(stored)

        def advance_one(fields):
            extended = jnp.pad(fields, ((0, 0), (1, 1), (0, 0), (0, 0)))
            return advance(fields, extended, coefficients)

        current = lax.map(advance_one, current)
    return current
```

```python
import functools

import jax
import jax.numpy as jnp
from jax import lax
from jax.experimental import pallas as pl
from jax.experimental.pallas import tpu as pltpu
from jax.sharding import PartitionSpec as P

STEPS = 2

SATURATION_SLOPE = 2.0
SHARPNESS = 4.0
CONDENSE_RATE = 0.25
LATENT_HEAT = 0.3

GROUP = 32
RING = 8


def spot(z, x, c):
    return (z % RING) * 4 + x * 2 + c


def shift_pattern(step, planes=range(RING)):
    return [
        (spot(z, x, c), spot(z + step, x, c)) for z in planes for x in range(2) for c in range(2)
    ]


X_PATTERN = [(i, i ^ 2) for i in range(GROUP)]
C_PATTERN = [(i, i ^ 1) for i in range(GROUP)]


def move(value, pattern):
    return lax.ppermute(value, "group", pattern)


def decode_slice(stored):
    decoded = stored.astype(jnp.float32)
    potential = 1.0 + 0.4 * decoded[4]
    exner_value = 1.0 + 0.4 * decoded[5]
    moisture = 1.0 + 2.0 * decoded[6]
    density = 1.0 + 0.8 * decoded[7]
    saturated = jnp.exp(SATURATION_SLOPE * (potential * exner_value - 1.0)) / density
    weight = jax.nn.sigmoid(SHARPNESS * (moisture - saturated))
    uptake = weight.astype(jnp.bfloat16)
    coupling = (weight * SATURATION_SLOPE * exner_value * saturated).astype(jnp.bfloat16)
    return lax.optimization_barrier(
        jnp.concatenate([stored[0:4], uptake[None], coupling[None]], axis=0)
    )


def step_kernel(edge_ref, q_ref, low_ref, high_ref, coef_ref, out_ref):
    planes, levels, width = q_ref.shape[1:]
    block = 16
    low_on, high_on = edge_ref[0], edge_ref[1]
    column = lax.broadcasted_iota(jnp.int32, (block, width), 1)
    row = lax.broadcasted_iota(jnp.int32, (block, width), 0)

    for plane in range(planes):
        for start in range(0, levels, block):
            rows = slice(start, start + block)
            speed = [coef_ref[k, plane, rows, :].astype(jnp.float32) for k in range(6)]
            diffusion = 0.025 + 0.06 * speed[3]
            west_w = jnp.maximum(speed[0], 0.0) + diffusion
            east_w = diffusion - jnp.minimum(speed[0], 0.0)
            south_w = jnp.maximum(speed[1], 0.0) + diffusion
            north_w = diffusion - jnp.minimum(speed[1], 0.0)
            below_w = jnp.maximum(speed[2], 0.0) + diffusion
            above_w = diffusion - jnp.minimum(speed[2], 0.0)
            centre_w = 1.0 - (west_w + east_w + south_w + north_w + below_w + above_w)
            south_w = jnp.where(column == 0, 0.0, south_w)
            north_w = jnp.where(column == width - 1, 0.0, north_w)
            if start == 0:
                below_w = jnp.where(row == 0, 0.0, below_w)
            if start + block == levels:
                above_w = jnp.where(row == block - 1, 0.0, above_w)
            if plane == 0:
                west_w = west_w * low_on
            if plane == planes - 1:
                east_w = east_w * high_on
            carried = []
            for field in range(4):
                centre = q_ref[field, plane, rows, :]
                if plane == 0:
                    west = low_ref[field, rows, :]
                else:
                    west = q_ref[field, plane - 1, rows, :]
                if plane == planes - 1:
                    east = high_ref[field, rows, :]
                else:
                    east = q_ref[field, plane + 1, rows, :]
                south = pltpu.roll(centre, 1, 1)
                north = pltpu.roll(centre, width - 1, 1)
                if start == 0:
                    below = pltpu.roll(centre, 1, 0)
                else:
                    below = q_ref[field, plane, start - 1 : start + block - 1, :]
                if start + block == levels:
                    above = pltpu.roll(centre, block - 1, 0)
                else:
                    above = q_ref[field, plane, start + 1 : start + block + 1, :]
                carried.append(
                    (centre_w * centre + west_w * west)
                    + (east_w * east + south_w * south)
                    + (north_w * north + below_w * below)
                    + above_w * above
                )
            condense = CONDENSE_RATE * (speed[4] * carried[1] - speed[5] * carried[0])
            out_ref[0, plane, rows, :] = carried[0] + LATENT_HEAT * condense
            out_ref[1, plane, rows, :] = carried[1] - condense
            out_ref[2, plane, rows, :] = carried[2] + condense
            out_ref[3, plane, rows, :] = carried[3]


def advance(fields, low, high, coefficients, edges):
    vmem = pl.BlockSpec(memory_space=pltpu.VMEM)
    return pl.pallas_call(
        step_kernel,
        out_shape=jax.ShapeDtypeStruct(fields.shape, jnp.float32),
        in_specs=[pl.BlockSpec(memory_space=pltpu.SMEM), vmem, vmem, vmem, vmem],
        out_specs=vmem,
        compiler_params=pltpu.CompilerParams(vmem_limit_bytes=24 * 1024 * 1024),
        cost_estimate=pl.CostEstimate(
            flops=8_000_000, bytes_accessed=4_000_000, transcendentals=0
        ),
    )(edges, fields, low, high, coefficients)


def ring_halo(fields):
    count = lax.axis_size("space")
    forward = [(i, (i + 1) % count) for i in range(count)]
    backward = [(target, source) for source, target in forward]
    low = lax.ppermute(fields[:, -1], "space", forward)
    high = lax.ppermute(fields[:, 0], "space", backward)
    return low, high


def pick(flag, yes, no):
    return jnp.where(flag, yes, no)


def ring_branch(classes):
    def spread(pieces, distance):
        far = []
        for piece, kind in zip(pieces, classes):
            sources = (kind, kind + 4)
            far.append(
                (
                    move(piece, shift_pattern(3, sources)),
                    move(piece, shift_pattern(-3, sources)),
                )
            )
        done = []
        for piece, (up, down), d in zip(pieces, far, distance):
            held = pick(d == 3, up, pick(d == 5, down, piece))
            plus = move(held, shift_pattern(1))
            minus = move(held, shift_pattern(-1))
            keep = (d == 0) | (d == 3) | (d == 5)
            from_low = (d == 1) | (d == 4) | (d == 6)
            done.append(pick(keep, held, pick(from_low, plus, minus)))
        return tuple(done)

    return spread


def on_device(perturbations, trajectory, slot_table, step_indices):
    fields = perturbations[0]
    me = lax.axis_index("group")
    my_z, my_x, my_c = me // 4, (me // 2) % 2, me % 2
    space = lax.axis_index("space")
    edges = jnp.stack([space > 0, space < lax.axis_size("space") - 1]).astype(jnp.float32)

    owners = [slot_table[step_indices[k]] for k in range(STEPS)]
    own_z = [o // 4 for o in owners]
    own_x = [(o // 2) % 2 for o in owners]
    own_c = [o % 2 for o in owners]
    distance = [(my_z - z) % RING for z in own_z]

    low, high = ring_halo(fields)

    coefficients = decode_slice(trajectory[0])
    shape = coefficients.shape
    rows = coefficients.reshape(2, 12, 64, 256)

    mine = lax.dynamic_index_in_dim(rows, my_c, 0, keepdims=False)
    other = move(lax.dynamic_index_in_dim(rows, 1 - my_c, 0, keepdims=False), C_PATTERN)
    pieces = []
    for k in range(STEPS):
        half = pick(own_c[k] == my_c, mine, other).reshape(2, 6, 64, 256)
        keep = lax.dynamic_index_in_dim(half, my_x, 0, keepdims=False)
        got = move(lax.dynamic_index_in_dim(half, 1 - my_x, 0, keepdims=False), X_PATTERN)
        pieces.append(pick(own_x[k] == my_x, keep, got))

    branches = [ring_branch((a, b)) for a in range(4) for b in range(4)]
    pieces = lax.switch(
        (own_z[0] % 4) * 4 + own_z[1] % 4, branches, tuple(pieces), tuple(distance)
    )

    for k in range(STEPS):
        piece = pieces[k]
        got = move(piece, X_PATTERN)
        half = jnp.concatenate(
            [pick(my_x == 0, piece, got), pick(my_x == 0, got, piece)], axis=0
        )
        got = move(half, C_PATTERN)
        whole = jnp.concatenate(
            [pick(my_c == 0, half, got), pick(my_c == 0, got, half)], axis=0
        ).reshape(shape)
        fields = advance(fields, low, high, whole, edges)
        if k + 1 < STEPS:
            low, high = ring_halo(fields)
    return fields[None]


def solution(mesh):
    return jax.shard_map(
        on_device,
        mesh=mesh,
        in_specs=(
            P("group", None, "space", None, None),
            P("group", None, "space", None, None),
            P(),
            P(),
        ),
        out_specs=P("group", None, "space", None, None),
        check_vma=False,
    )
```

```python
import functools

import jax
import jax.numpy as jnp
from jax import lax
from jax.experimental import pallas as pl
from jax.experimental.pallas import tpu as pltpu
from jax.sharding import PartitionSpec as P

STEPS = 2

SATURATION_SLOPE = 2.0
SHARPNESS = 4.0
CONDENSE_RATE = 0.25
LATENT_HEAT = 0.3

GROUP = 32
RING = 8


def spot(z, x, c):
    return (z % RING) * 4 + x * 2 + c


def shift_pattern(step, planes=range(RING)):
    return [
        (spot(z, x, c), spot(z + step, x, c)) for z in planes for x in range(2) for c in range(2)
    ]


X_PATTERN = [(i, i ^ 2) for i in range(GROUP)]
C_PATTERN = [(i, i ^ 1) for i in range(GROUP)]


def move(value, pattern):
    return lax.ppermute(value, "group", pattern)


def decode_kernel(
    stored_hbm, table_hbm, steps_hbm, fields_hbm,
    keep_ref, send_ref, first_ref, last_ref, owner_ref,
    stored_ref, table_ref, steps_ref, edge_ref, sems,
):
    small = [
        pltpu.make_async_copy(table_hbm, table_ref, sems.at[4]),
        pltpu.make_async_copy(steps_hbm, steps_ref, sems.at[5]),
    ]
    copies = [
        pltpu.make_async_copy(stored_hbm.at[0, :, p], stored_ref.at[p], sems.at[p]) for p in range(4)
    ]
    sides = [
        pltpu.make_async_copy(fields_hbm.at[0, :, 3 * k], edge_ref.at[k], sems.at[6 + k])
        for k in range(2)
    ]
    for copy in small + copies + sides:
        copy.start()
    first = lax.rem(lax.axis_index("group"), 2) == 0
    for p in range(4):
        copies[p].wait()
        for start in range(0, 64, 32):
            rows = slice(start, start + 32)
            potential, exner_value, moisture, density = (
                1.0 + scale * stored_ref[p, k, rows, :].astype(jnp.float32)
                for k, scale in ((4, 0.4), (5, 0.4), (6, 2.0), (7, 0.8))
            )
            saturated = jnp.exp(SATURATION_SLOPE * (potential * exner_value - 1.0)) / density
            weight = jax.nn.sigmoid(SHARPNESS * (moisture - saturated))
            uptake = weight.astype(jnp.bfloat16)
            coupling = (weight * SATURATION_SLOPE * exner_value * saturated).astype(jnp.bfloat16)
            low = [stored_ref[p, k, rows, :] for k in range(3)]
            high = [stored_ref[p, 3, rows, :], uptake, coupling]
            for k in range(3):
                keep_ref[4 * k + p, rows, :] = jnp.where(first, low[k], high[k])
                send_ref[4 * k + p, rows, :] = jnp.where(first, high[k], low[k])
    for k, target in enumerate((first_ref, last_ref)):
        sides[k].wait()
        target[...] = edge_ref[k].astype(jnp.bfloat16)
    for copy in small:
        copy.wait()
    owner_ref[0] = table_ref[steps_ref[0]] + GROUP * table_ref[steps_ref[1]]


def decode_slice(trajectory, slot_table, step_indices, perturbations):
    vmem = pl.BlockSpec(memory_space=pltpu.VMEM)
    half = jax.ShapeDtypeStruct((12, 64, 256), jnp.bfloat16)
    edge = jax.ShapeDtypeStruct((4, 64, 256), jnp.bfloat16)
    return pl.pallas_call(
        decode_kernel,
        out_shape=(half, half, edge, edge, jax.ShapeDtypeStruct((1,), jnp.int32)),
        in_specs=[pl.BlockSpec(memory_space=pltpu.HBM)] * 4,
        out_specs=(vmem, vmem, vmem, vmem, pl.BlockSpec(memory_space=pltpu.SMEM)),
        scratch_shapes=[
            pltpu.VMEM((4, 8, 64, 256), jnp.bfloat16),
            pltpu.SMEM((GROUP,), jnp.int32),
            pltpu.SMEM((STEPS,), jnp.int32),
            pltpu.VMEM((2, 4, 64, 256), jnp.float32),
            pltpu.SemaphoreType.DMA((8,)),
        ],
        compiler_params=pltpu.CompilerParams(vmem_limit_bytes=56 * 1024 * 1024),
        cost_estimate=pl.CostEstimate(
            flops=1_500_000, bytes_accessed=2_800_000, transcendentals=200_000
        ),
    )(trajectory, slot_table, step_indices, perturbations)


def step_kernel(edge_ref, q_ref, low_ref, high_ref, coef_ref, out_ref):
    planes, levels, width = q_ref.shape[1:]
    block = 16
    low_on, high_on = edge_ref[0], edge_ref[1]
    column = lax.broadcasted_iota(jnp.int32, (block, width), 1)
    row = lax.broadcasted_iota(jnp.int32, (block, width), 0)

    for plane in range(planes):
        for start in range(0, levels, block):
            rows = slice(start, start + block)
            speed = [coef_ref[k, plane, rows, :].astype(jnp.float32) for k in range(6)]
            diffusion = 0.025 + 0.06 * speed[3]
            west_w = jnp.maximum(speed[0], 0.0) + diffusion
            east_w = diffusion - jnp.minimum(speed[0], 0.0)
            south_w = jnp.maximum(speed[1], 0.0) + diffusion
            north_w = diffusion - jnp.minimum(speed[1], 0.0)
            below_w = jnp.maximum(speed[2], 0.0) + diffusion
            above_w = diffusion - jnp.minimum(speed[2], 0.0)
            centre_w = 1.0 - (west_w + east_w + south_w + north_w + below_w + above_w)
            south_w = jnp.where(column == 0, 0.0, south_w)
            north_w = jnp.where(column == width - 1, 0.0, north_w)
            if start == 0:
                below_w = jnp.where(row == 0, 0.0, below_w)
            if start + block == levels:
                above_w = jnp.where(row == block - 1, 0.0, above_w)
            if plane == 0:
                west_w = west_w * low_on
            if plane == planes - 1:
                east_w = east_w * high_on
            carried = []
            for field in range(4):
                centre = q_ref[field, plane, rows, :]
                if plane == 0:
                    west = low_ref[field, rows, :].astype(jnp.float32)
                else:
                    west = q_ref[field, plane - 1, rows, :]
                if plane == planes - 1:
                    east = high_ref[field, rows, :].astype(jnp.float32)
                else:
                    east = q_ref[field, plane + 1, rows, :]
                south = pltpu.roll(centre, 1, 1)
                north = pltpu.roll(centre, width - 1, 1)
                if start == 0:
                    below = pltpu.roll(centre, 1, 0)
                else:
                    below = q_ref[field, plane, start - 1 : start + block - 1, :]
                if start + block == levels:
                    above = pltpu.roll(centre, block - 1, 0)
                else:
                    above = q_ref[field, plane, start + 1 : start + block + 1, :]
                carried.append(
                    (centre_w * centre + west_w * west)
                    + (east_w * east + south_w * south)
                    + (north_w * north + below_w * below)
                    + above_w * above
                )
            condense = CONDENSE_RATE * (speed[4] * carried[1] - speed[5] * carried[0])
            out_ref[0, plane, rows, :] = carried[0] + LATENT_HEAT * condense
            out_ref[1, plane, rows, :] = carried[1] - condense
            out_ref[2, plane, rows, :] = carried[2] + condense
            out_ref[3, plane, rows, :] = carried[3]


def advance(fields, low, high, coefficients, edges):
    vmem = pl.BlockSpec(memory_space=pltpu.VMEM)
    return pl.pallas_call(
        step_kernel,
        out_shape=jax.ShapeDtypeStruct(fields.shape, jnp.float32),
        in_specs=[pl.BlockSpec(memory_space=pltpu.SMEM), vmem, vmem, vmem, vmem],
        out_specs=vmem,
        compiler_params=pltpu.CompilerParams(vmem_limit_bytes=24 * 1024 * 1024),
        cost_estimate=pl.CostEstimate(
            flops=8_000_000, bytes_accessed=4_000_000, transcendentals=0
        ),
    )(edges, fields, low, high, coefficients)


def ring_patterns():
    count = lax.axis_size("space")
    forward = [(i, (i + 1) % count) for i in range(count)]
    return forward, [(target, source) for source, target in forward]


def ring_halo(first, last):
    forward, backward = ring_patterns()
    return lax.ppermute(last, "space", forward), lax.ppermute(first, "space", backward)


def pick(flag, yes, no):
    return jnp.where(flag, yes, no)


def far_branch(plane):
    def send(piece):
        return move(piece, shift_pattern(3, [plane])), move(piece, shift_pattern(-3, [plane]))

    return send


def far(piece, plane, distance):
    up, down = lax.switch(plane, [far_branch(p) for p in range(RING)], piece)
    return pick(distance == 3, up, pick(distance == 5, down, piece))


def near(held, distance):
    plus = move(held, shift_pattern(1))
    minus = move(held, shift_pattern(-1))
    keep = (distance == 0) | (distance == 3) | (distance == 5)
    from_low = (distance == 1) | (distance == 4) | (distance == 6)
    return pick(keep, held, pick(from_low, plus, minus))


def on_device(perturbations, trajectory, slot_table, step_indices):
    fields = perturbations[0]
    me = lax.axis_index("group")
    my_z, my_x, my_c = me // 4, (me // 2) % 2, me % 2
    space = lax.axis_index("space")
    edges = jnp.stack([space > 0, space < lax.axis_size("space") - 1]).astype(jnp.float32)

    mine, sent, first, last, packed = decode_slice(
        trajectory, slot_table, step_indices, perturbations
    )
    other = move(sent, C_PATTERN)
    packed = packed[0]
    owners = [packed % GROUP, packed // GROUP]
    planes = [owner // 4 for owner in owners]
    distance = [(my_z - z) % RING for z in planes]
    low, high = ring_halo(first, last)

    pieces = []
    for k, owner in enumerate(owners):
        half = pick(owner % 2 == my_c, mine, other).reshape(2, 6, 64, 256)
        keep = lax.dynamic_index_in_dim(half, my_x, 0, keepdims=False)
        got = move(lax.dynamic_index_in_dim(half, 1 - my_x, 0, keepdims=False), X_PATTERN)
        pieces.append(pick((owner // 2) % 2 == my_x, keep, got))
    pieces[1], low, high = lax.optimization_barrier((pieces[1], low, high))
    pieces = [
        near(far(piece, z, d), d) for piece, z, d in zip(pieces, planes, distance)
    ]

    for k in range(STEPS):
        piece = pieces[k]
        got = move(piece, X_PATTERN)
        half = jnp.concatenate(
            [pick(my_x == 0, piece, got), pick(my_x == 0, got, piece)], axis=0
        )
        got = move(half, C_PATTERN)
        whole = jnp.concatenate(
            [pick(my_c == 0, half, got), pick(my_c == 0, got, half)], axis=0
        ).reshape(6, 4, 64, 256)
        fields = advance(fields, low, high, whole, edges)
        if k + 1 < STEPS:
            low, high = ring_halo(
                fields[:, 0].astype(jnp.bfloat16), fields[:, -1].astype(jnp.bfloat16)
            )
    return fields[None]


def solution(mesh):
    return jax.shard_map(
        on_device,
        mesh=mesh,
        in_specs=(
            P("group", None, "space", None, None),
            P("group", None, "space", None, None),
            P(),
            P(),
        ),
        out_specs=P("group", None, "space", None, None),
        check_vma=False,
    )
```

```python
import jax
import jax.numpy as jnp
from jax import lax
from jax.experimental import pallas as pl
from jax.experimental.pallas import tpu as pltpu
from jax.sharding import PartitionSpec as P

STEPS = 2

SATURATION_SLOPE = 2.0
SHARPNESS = 4.0
CONDENSE_RATE = 0.25
LATENT_HEAT = 0.3

GROUP = 32
RING = 8
SPACE = 8
PLANES, LEVELS, WIDTH = 4, 64, 256
BLOCK = 16
MIB = 1024 * 1024

VMEM = pl.BlockSpec(memory_space=pltpu.VMEM)
SMEM = pl.BlockSpec(memory_space=pltpu.SMEM)
HBM = pl.BlockSpec(memory_space=pltpu.HBM)


def spot(z, x, c):
    return (z % RING) * 4 + x * 2 + c


def shift_pattern(step, planes=range(RING)):
    return [
        (spot(z, x, c), spot(z + step, x, c)) for z in planes for x in range(2) for c in range(2)
    ]


X_PATTERN = [(i, i ^ 2) for i in range(GROUP)]
C_PATTERN = [(i, i ^ 1) for i in range(GROUP)]
FORWARD = [(i, (i + 1) % SPACE) for i in range(SPACE)]
BACKWARD = [(target, source) for source, target in FORWARD]


def move(value, pattern):
    return lax.ppermute(value, "group", pattern)


def pick(flag, yes, no):
    return jnp.where(flag, yes, no)


def decode_kernel(
    stored_hbm, table_hbm, steps_hbm, fields_hbm,
    keep_ref, send_ref, bottom_ref, top_ref, owner_ref,
    stored_ref, table_ref, steps_ref, edge_ref, sems,
):
    small = [
        pltpu.make_async_copy(table_hbm, table_ref, sems.at[4]),
        pltpu.make_async_copy(steps_hbm, steps_ref, sems.at[5]),
    ]
    copies = [
        pltpu.make_async_copy(stored_hbm.at[0, :, p], stored_ref.at[p], sems.at[p])
        for p in range(PLANES)
    ]
    sides = [
        pltpu.make_async_copy(fields_hbm.at[0, :, 3 * k], edge_ref.at[k], sems.at[6 + k])
        for k in range(2)
    ]
    for copy in small + copies + sides:
        copy.start()
    mine = lax.rem(lax.axis_index("group"), 2)
    for p in range(PLANES):
        copies[p].wait()
        values = []
        for start in range(0, LEVELS, 32):
            rows = slice(start, start + 32)
            potential, exner_value, moisture, density = (
                1.0 + scale * stored_ref[p, k, rows, :].astype(jnp.float32)
                for k, scale in ((4, 0.4), (5, 0.4), (6, 2.0), (7, 0.8))
            )
            saturated = jnp.exp(SATURATION_SLOPE * (potential * exner_value - 1.0)) / density
            weight = jax.nn.sigmoid(SHARPNESS * (moisture - saturated))
            uptake = weight.astype(jnp.bfloat16)
            coupling = (weight * SATURATION_SLOPE * exner_value * saturated).astype(jnp.bfloat16)
            stored_ref[p, 4, rows, :] = uptake
            stored_ref[p, 5, rows, :] = coupling

        @pl.when(mine == p // 2)
        def _():
            keep_ref[p % 2] = stored_ref[p, 0:6]

        @pl.when(mine != p // 2)
        def _():
            send_ref[p % 2] = stored_ref[p, 0:6]

    for k, target in enumerate((bottom_ref, top_ref)):
        sides[k].wait()
        target[...] = edge_ref[k].astype(jnp.bfloat16)
    for copy in small:
        copy.wait()
    owner_ref[0] = table_ref[steps_ref[0]] + GROUP * table_ref[steps_ref[1]]


def decode_slice(trajectory, slot_table, step_indices, perturbations):
    half = jax.ShapeDtypeStruct((2, 6, LEVELS, WIDTH), jnp.bfloat16)
    edge = jax.ShapeDtypeStruct((4, LEVELS, WIDTH), jnp.bfloat16)
    return pl.pallas_call(
        decode_kernel,
        out_shape=(half, half, edge, edge, jax.ShapeDtypeStruct((1,), jnp.int32)),
        in_specs=[HBM] * 4,
        out_specs=(VMEM, VMEM, VMEM, VMEM, SMEM),
        scratch_shapes=[
            pltpu.VMEM((PLANES, 8, LEVELS, WIDTH), jnp.bfloat16),
            pltpu.SMEM((GROUP,), jnp.int32),
            pltpu.SMEM((STEPS,), jnp.int32),
            pltpu.VMEM((2, 4, LEVELS, WIDTH), jnp.float32),
            pltpu.SemaphoreType.DMA((8,)),
        ],
        compiler_params=pltpu.CompilerParams(vmem_limit_bytes=56 * MIB),
        cost_estimate=pl.CostEstimate(
            flops=1_500_000, bytes_accessed=3_500_000, transcendentals=200_000
        ),
    )(trajectory, slot_table, step_indices, perturbations)


def stencil(coef, centre, west, east, out, west_on=None, east_on=None):
    column = lax.broadcasted_iota(jnp.int32, (BLOCK, WIDTH), 1)
    row = lax.broadcasted_iota(jnp.int32, (BLOCK, WIDTH), 0)
    for start in range(0, LEVELS, BLOCK):
        rows = slice(start, start + BLOCK)
        speed = [coef(k, rows).astype(jnp.float32) for k in range(6)]
        diffusion = 0.025 + 0.06 * speed[3]
        west_w = jnp.maximum(speed[0], 0.0) + diffusion
        east_w = diffusion - jnp.minimum(speed[0], 0.0)
        south_w = jnp.maximum(speed[1], 0.0) + diffusion
        north_w = diffusion - jnp.minimum(speed[1], 0.0)
        below_w = jnp.maximum(speed[2], 0.0) + diffusion
        above_w = diffusion - jnp.minimum(speed[2], 0.0)
        centre_w = 1.0 - (west_w + east_w + south_w + north_w + below_w + above_w)
        south_w = jnp.where(column == 0, 0.0, south_w)
        north_w = jnp.where(column == WIDTH - 1, 0.0, north_w)
        if start == 0:
            below_w = jnp.where(row == 0, 0.0, below_w)
        if start + BLOCK == LEVELS:
            above_w = jnp.where(row == BLOCK - 1, 0.0, above_w)
        if west_on is not None:
            west_w = west_w * west_on
        if east_on is not None:
            east_w = east_w * east_on
        carried = []
        for field in range(4):
            here = centre(field, rows)
            if start == 0:
                below = pltpu.roll(here, 1, 0)
            else:
                below = centre(field, slice(start - 1, start + BLOCK - 1))
            if start + BLOCK == LEVELS:
                above = pltpu.roll(here, BLOCK - 1, 0)
            else:
                above = centre(field, slice(start + 1, start + BLOCK + 1))
            carried.append(
                (centre_w * here + west_w * west(field, rows))
                + (east_w * east(field, rows) + south_w * pltpu.roll(here, 1, 1))
                + (north_w * pltpu.roll(here, WIDTH - 1, 1) + below_w * below)
                + above_w * above
            )
        condense = CONDENSE_RATE * (speed[4] * carried[1] - speed[5] * carried[0])
        out(0, rows, carried[0] + LATENT_HEAT * condense)
        out(1, rows, carried[1] - condense)
        out(2, rows, carried[2] + condense)
        out(3, rows, carried[3])


def reader(ref, plane):
    return lambda field, rows: ref[field, plane, rows, :].astype(jnp.float32)


def writer(ref, plane):
    def write(field, rows, value):
        ref[field, plane, rows, :] = value

    return write


def coefficient(ref, plane):
    return lambda k, rows: ref[plane, k, rows, :]


def edge_reader(ref):
    return lambda field, rows: ref[field, rows, :].astype(jnp.float32)


def slab(on_ref, q_ref, high_ref, low_ref, coef_ref, out_ref, done=lambda p: None):
    for p in range(PLANES):
        stencil(
            coefficient(coef_ref, p),
            reader(q_ref, p),
            reader(q_ref, p - 1) if p else edge_reader(low_ref),
            reader(q_ref, p + 1) if p + 1 < PLANES else edge_reader(high_ref),
            writer(out_ref, p),
            on_ref[0] if p == 0 else None,
            on_ref[1] if p + 1 == PLANES else None,
        )
        done(p)


def second_kernel(on_ref, q_ref, high_ref, low_ref, coef_ref, out_hbm, out_ref, sems):
    copies = [
        pltpu.make_async_copy(out_ref.at[:, p], out_hbm.at[:, p], sems.at[p])
        for p in range(PLANES)
    ]
    slab(on_ref, q_ref, high_ref, low_ref, coef_ref, out_ref, lambda p: copies[p].start())
    for copy in copies:
        copy.wait()


def step(kernel, out_spec, scratch, arrays):
    return pl.pallas_call(
        kernel,
        out_shape=jax.ShapeDtypeStruct((4, PLANES, LEVELS, WIDTH), jnp.float32),
        in_specs=[SMEM] + [VMEM] * 4,
        out_specs=out_spec,
        scratch_shapes=scratch,
        compiler_params=pltpu.CompilerParams(vmem_limit_bytes=24 * MIB),
        cost_estimate=pl.CostEstimate(
            flops=8_000_000, bytes_accessed=4_000_000, transcendentals=0
        ),
    )(*arrays)


def first_step(*arrays):
    return step(slab, VMEM, [], arrays)


def second_step(*arrays):
    scratch = [
        pltpu.VMEM((4, PLANES, LEVELS, WIDTH), jnp.float32),
        pltpu.SemaphoreType.DMA((PLANES,)),
    ]
    return step(second_kernel, HBM, scratch, arrays)


def far_branch(plane):
    def send(piece):
        return move(piece, shift_pattern(3, [plane])), move(piece, shift_pattern(-3, [plane]))

    return send


def far(piece, plane, distance):
    up, down = lax.switch(plane, [far_branch(p) for p in range(RING)], piece)
    return pick(distance == 3, up, pick(distance == 5, down, piece))


def near_moves(held):
    return move(held, shift_pattern(1)), move(held, shift_pattern(-1))


def near_pick(held, plus, minus, distance):
    keep = (distance == 0) | (distance == 3) | (distance == 5)
    from_low = (distance == 1) | (distance == 4) | (distance == 6)
    return pick(keep, held, pick(from_low, plus, minus))


def ordered(flag, own, got):
    return jnp.stack([pick(flag, got, own), pick(flag, own, got)])


def on_device(perturbations, trajectory, slot_table, step_indices):
    me = lax.axis_index("group")
    my_z, my_x, my_c = me // 4, (me // 2) % 2, me % 2
    space = lax.axis_index("space")
    on = jnp.stack([space > 0, space < SPACE - 1]).astype(jnp.float32)

    mine, sent, bottom, top, packed = decode_slice(
        trajectory, slot_table, step_indices, perturbations
    )
    other = move(sent, C_PATTERN)
    packed = packed[0]
    owners = [packed % GROUP, packed // GROUP]
    planes = [owner // 4 for owner in owners]
    distance = [(my_z - z) % RING for z in planes]
    low = lax.ppermute(top, "space", FORWARD)
    high = lax.ppermute(bottom, "space", BACKWARD)

    fields = perturbations[0]
    waiting = []
    for owner in owners:
        half = pick(owner % 2 == my_c, mine, other)
        keep = lax.dynamic_index_in_dim(half, my_x, 0, keepdims=False)
        got = move(lax.dynamic_index_in_dim(half, 1 - my_x, 0, keepdims=False), X_PATTERN)
        waiting.append((keep, got))
    pieces = [
        pick((owner // 2) % 2 == my_x, keep, got) for owner, (keep, got) in zip(owners, waiting)
    ]

    first = far(pieces[0], planes[0], distance[0])
    first_moves = near_moves(first)
    second, low, high = lax.optimization_barrier((pieces[1], low, high))
    second = far(second, planes[1], distance[1])
    second, first_moves = lax.optimization_barrier((second, first_moves))
    first = near_pick(first, *first_moves, distance[0])
    pair = ordered(my_x == 1, first, move(first, X_PATTERN))
    second = near_pick(second, *near_moves(second), distance[1])
    got, other = move(second, X_PATTERN), move(pair, C_PATTERN)
    whole = ordered(my_c == 1, pair, other).reshape(PLANES, 6, LEVELS, WIDTH)
    fields = first_step(on, fields, high, low, whole)
    got, _ = lax.optimization_barrier((got, fields))
    low = lax.ppermute(fields[:, -1].astype(jnp.bfloat16), "space", FORWARD)
    high = lax.ppermute(fields[:, 0].astype(jnp.bfloat16), "space", BACKWARD)
    pair = ordered(my_x == 1, second, got)
    whole = ordered(my_c == 1, pair, move(pair, C_PATTERN)).reshape(PLANES, 6, LEVELS, WIDTH)
    return second_step(on, fields, high, low, whole)[None]


def solution(mesh):
    return jax.shard_map(
        on_device,
        mesh=mesh,
        in_specs=(
            P("group", None, "space", None, None),
            P("group", None, "space", None, None),
            P(),
            P(),
        ),
        out_specs=P("group", None, "space", None, None),
        check_vma=False,
    )
```

```python
import jax
import jax.numpy as jnp
from jax import lax
from jax.experimental import pallas as pl
from jax.experimental.pallas import tpu as pltpu
from jax.sharding import Mesh
from jax.sharding import PartitionSpec as P

STEPS = 2

SATURATION_SLOPE = 2.0
SHARPNESS = 4.0
CONDENSE_RATE = 0.25
LATENT_HEAT = 0.3

GROUP = 32
RING = 8
SPACE = 8
GROUP_AXES = ("z", "x", "c")
PLANES, LEVELS, WIDTH = 4, 64, 256
BLOCK = 16
MIB = 1024 * 1024

VMEM = pl.BlockSpec(memory_space=pltpu.VMEM)
SMEM = pl.BlockSpec(memory_space=pltpu.SMEM)
HBM = pl.BlockSpec(memory_space=pltpu.HBM)


def spot(z, x, c):
    return (z % RING) * 4 + x * 2 + c


def shift_pattern(step, planes=range(RING)):
    return [
        (spot(z, x, c), spot(z + step, x, c)) for z in planes for x in range(2) for c in range(2)
    ]


X_PATTERN = [(i, i ^ 2) for i in range(GROUP)]
C_PATTERN = [(i, i ^ 1) for i in range(GROUP)]
FORWARD = [(i, (i + 1) % SPACE) for i in range(SPACE)]
BACKWARD = [(target, source) for source, target in FORWARD]


def move(value, pattern):
    return lax.ppermute(value, GROUP_AXES, pattern)


def pick(flag, yes, no):
    return jnp.where(flag, yes, no)


def decode_kernel(
    stored_hbm, table_hbm, steps_hbm, fields_hbm,
    keep_ref, send_ref, bottom_ref, top_ref, owner_ref,
    stored_ref, table_ref, steps_ref, edge_ref, sems,
):
    small = [
        pltpu.make_async_copy(table_hbm, table_ref, sems.at[4]),
        pltpu.make_async_copy(steps_hbm, steps_ref, sems.at[5]),
    ]
    copies = [
        pltpu.make_async_copy(stored_hbm.at[0, :, p], stored_ref.at[p], sems.at[p])
        for p in range(PLANES)
    ]
    sides = [
        pltpu.make_async_copy(fields_hbm.at[0, :, 3 * k], edge_ref.at[k], sems.at[6 + k])
        for k in range(2)
    ]
    for copy in small + copies + sides:
        copy.start()
    mine = lax.axis_index("c")
    for p in range(PLANES):
        copies[p].wait()
        values = []
        for start in range(0, LEVELS, 32):
            rows = slice(start, start + 32)
            potential, exner_value, moisture, density = (
                1.0 + scale * stored_ref[p, k, rows, :].astype(jnp.float32)
                for k, scale in ((4, 0.4), (5, 0.4), (6, 2.0), (7, 0.8))
            )
            saturated = jnp.exp(SATURATION_SLOPE * (potential * exner_value - 1.0)) / density
            weight = jax.nn.sigmoid(SHARPNESS * (moisture - saturated))
            uptake = weight.astype(jnp.bfloat16)
            coupling = (weight * SATURATION_SLOPE * exner_value * saturated).astype(jnp.bfloat16)
            stored_ref[p, 4, rows, :] = uptake
            stored_ref[p, 5, rows, :] = coupling

        @pl.when(mine == p // 2)
        def _():
            keep_ref[p % 2] = stored_ref[p, 0:6]

        @pl.when(mine != p // 2)
        def _():
            send_ref[p % 2] = stored_ref[p, 0:6]

    for k, target in enumerate((bottom_ref, top_ref)):
        sides[k].wait()
        target[...] = edge_ref[k].astype(jnp.bfloat16)
    for copy in small:
        copy.wait()
    owner_ref[0] = table_ref[steps_ref[0]] + GROUP * table_ref[steps_ref[1]]


def decode_slice(trajectory, slot_table, step_indices, perturbations):
    half = jax.ShapeDtypeStruct((2, 6, LEVELS, WIDTH), jnp.bfloat16)
    edge = jax.ShapeDtypeStruct((4, LEVELS, WIDTH), jnp.bfloat16)
    return pl.pallas_call(
        decode_kernel,
        out_shape=(half, half, edge, edge, jax.ShapeDtypeStruct((1,), jnp.int32)),
        in_specs=[HBM] * 4,
        out_specs=(VMEM, VMEM, VMEM, VMEM, SMEM),
        scratch_shapes=[
            pltpu.VMEM((PLANES, 8, LEVELS, WIDTH), jnp.bfloat16),
            pltpu.SMEM((GROUP,), jnp.int32),
            pltpu.SMEM((STEPS,), jnp.int32),
            pltpu.VMEM((2, 4, LEVELS, WIDTH), jnp.float32),
            pltpu.SemaphoreType.DMA((8,)),
        ],
        compiler_params=pltpu.CompilerParams(vmem_limit_bytes=56 * MIB),
        cost_estimate=pl.CostEstimate(
            flops=1_500_000, bytes_accessed=3_500_000, transcendentals=200_000
        ),
    )(trajectory, slot_table, step_indices, perturbations)


def stencil(coef, centre, west, east, out, west_on=None, east_on=None):
    column = lax.broadcasted_iota(jnp.int32, (BLOCK, WIDTH), 1)
    row = lax.broadcasted_iota(jnp.int32, (BLOCK, WIDTH), 0)
    for start in range(0, LEVELS, BLOCK):
        rows = slice(start, start + BLOCK)
        speed = [coef(k, rows).astype(jnp.float32) for k in range(6)]
        diffusion = 0.025 + 0.06 * speed[3]
        west_w = jnp.maximum(speed[0], 0.0) + diffusion
        east_w = diffusion - jnp.minimum(speed[0], 0.0)
        south_w = jnp.maximum(speed[1], 0.0) + diffusion
        north_w = diffusion - jnp.minimum(speed[1], 0.0)
        below_w = jnp.maximum(speed[2], 0.0) + diffusion
        above_w = diffusion - jnp.minimum(speed[2], 0.0)
        centre_w = 1.0 - (west_w + east_w + south_w + north_w + below_w + above_w)
        south_w = jnp.where(column == 0, 0.0, south_w)
        north_w = jnp.where(column == WIDTH - 1, 0.0, north_w)
        if start == 0:
            below_w = jnp.where(row == 0, 0.0, below_w)
        if start + BLOCK == LEVELS:
            above_w = jnp.where(row == BLOCK - 1, 0.0, above_w)
        if west_on is not None:
            west_w = west_w * west_on
        if east_on is not None:
            east_w = east_w * east_on
        carried = []
        for field in range(4):
            here = centre(field, rows)
            if start == 0:
                below = pltpu.roll(here, 1, 0)
            else:
                below = centre(field, slice(start - 1, start + BLOCK - 1))
            if start + BLOCK == LEVELS:
                above = pltpu.roll(here, BLOCK - 1, 0)
            else:
                above = centre(field, slice(start + 1, start + BLOCK + 1))
            carried.append(
                (centre_w * here + west_w * west(field, rows))
                + (east_w * east(field, rows) + south_w * pltpu.roll(here, 1, 1))
                + (north_w * pltpu.roll(here, WIDTH - 1, 1) + below_w * below)
                + above_w * above
            )
        condense = CONDENSE_RATE * (speed[4] * carried[1] - speed[5] * carried[0])
        out(0, rows, carried[0] + LATENT_HEAT * condense)
        out(1, rows, carried[1] - condense)
        out(2, rows, carried[2] + condense)
        out(3, rows, carried[3])


def reader(ref, plane):
    return lambda field, rows: ref[field, plane, rows, :].astype(jnp.float32)


def writer(ref, plane):
    def write(field, rows, value):
        ref[field, plane, rows, :] = value

    return write


def coefficient(ref, plane):
    return lambda k, rows: ref[plane, k, rows, :]


def edge_reader(ref):
    return lambda field, rows: ref[field, rows, :].astype(jnp.float32)


def pair_reader(ref, k):
    return lambda field, rows: ref[k, field, rows, :].astype(jnp.float32)


def both_writer(ref, narrow_ref, k):
    def write(field, rows, value):
        ref[k, field, rows, :] = value
        narrow_ref[k, field, rows, :] = value.astype(jnp.bfloat16)

    return write


def pair_writer(ref, k):
    def write(field, rows, value):
        ref[k, field, rows, :] = value

    return write


def first_outer(on_ref, q_ref, high_ref, low_ref, coef_ref, out_ref, narrow_ref):
    stencil(
        coefficient(coef_ref, 0), reader(q_ref, 0), edge_reader(low_ref), reader(q_ref, 1),
        both_writer(out_ref, narrow_ref, 0), west_on=on_ref[0],
    )
    stencil(
        coefficient(coef_ref, 3), reader(q_ref, 3), reader(q_ref, 2), edge_reader(high_ref),
        both_writer(out_ref, narrow_ref, 1), east_on=on_ref[1],
    )


def first_inner(q_ref, coef_ref, out_ref):
    for p in (1, 2):
        stencil(
            coefficient(coef_ref, p), reader(q_ref, p), reader(q_ref, p - 1), reader(q_ref, p + 1),
            pair_writer(out_ref, p - 1),
        )


def second_inner(outer_ref, inner_ref, coef_ref, out_hbm, out_ref, sems):
    planes = [pair_reader(outer_ref, 0), pair_reader(inner_ref, 0), pair_reader(inner_ref, 1), pair_reader(outer_ref, 1)]
    copies = []
    for p in (1, 2):
        stencil(
            coefficient(coef_ref, p), planes[p], planes[p - 1], planes[p + 1],
            pair_writer(out_ref, p - 1),
        )
        copies.append(pltpu.make_async_copy(out_ref.at[p - 1], out_hbm.at[:, p], sems.at[p - 1]))
        copies[-1].start()
    for copy in copies:
        copy.wait()


def second_outer(
    on_ref, outer_ref, inner_ref, high_ref, low_ref, coef_ref, part_hbm, out_hbm, out_ref, sems
):
    stencil(
        coefficient(coef_ref, 0), pair_reader(outer_ref, 0), edge_reader(low_ref),
        pair_reader(inner_ref, 0), pair_writer(out_ref, 0), west_on=on_ref[0],
    )
    low_copy = pltpu.make_async_copy(out_ref.at[0], out_hbm.at[:, 0], sems.at[0])
    low_copy.start()
    stencil(
        coefficient(coef_ref, 3), pair_reader(outer_ref, 1), pair_reader(inner_ref, 1),
        edge_reader(high_ref), pair_writer(out_ref, 1), east_on=on_ref[1],
    )
    high_copy = pltpu.make_async_copy(out_ref.at[1], out_hbm.at[:, 3], sems.at[1])
    high_copy.start()
    low_copy.wait()
    high_copy.wait()


PAIR = (2, 4, LEVELS, WIDTH)
WHOLE = jax.ShapeDtypeStruct((4, PLANES, LEVELS, WIDTH), jnp.float32)
COST = pl.CostEstimate(flops=4_000_000, bytes_accessed=3_000_000, transcendentals=0)
PARAMS = pltpu.CompilerParams(vmem_limit_bytes=16 * MIB)


def first_outer_step(*arrays):
    return pl.pallas_call(
        first_outer,
        out_shape=(
            jax.ShapeDtypeStruct(PAIR, jnp.float32),
            jax.ShapeDtypeStruct(PAIR, jnp.bfloat16),
        ),
        in_specs=[SMEM] + [VMEM] * 4,
        out_specs=(VMEM, VMEM),
        compiler_params=PARAMS,
        cost_estimate=COST,
    )(*arrays)


def first_inner_step(*arrays):
    return pl.pallas_call(
        first_inner,
        out_shape=jax.ShapeDtypeStruct(PAIR, jnp.float32),
        in_specs=[VMEM] * 2,
        out_specs=VMEM,
        compiler_params=PARAMS,
        cost_estimate=COST,
    )(*arrays)


def second_inner_step(*arrays):
    return pl.pallas_call(
        second_inner,
        out_shape=WHOLE,
        in_specs=[VMEM] * 3,
        out_specs=HBM,
        scratch_shapes=[pltpu.VMEM(PAIR, jnp.float32), pltpu.SemaphoreType.DMA((2,))],
        compiler_params=PARAMS,
        cost_estimate=COST,
    )(*arrays)


def second_outer_step(*arrays):
    return pl.pallas_call(
        second_outer,
        out_shape=WHOLE,
        in_specs=[SMEM] + [VMEM] * 5 + [HBM],
        out_specs=HBM,
        scratch_shapes=[pltpu.VMEM(PAIR, jnp.float32), pltpu.SemaphoreType.DMA((2,))],
        input_output_aliases={6: 0},
        compiler_params=PARAMS,
        cost_estimate=COST,
    )(*arrays)


def load_kernel(source_hbm, target_ref, sem):
    copy = pltpu.make_async_copy(source_hbm, target_ref, sem)
    copy.start()
    copy.wait()


def load(fields):
    return pl.pallas_call(
        load_kernel,
        out_shape=WHOLE,
        in_specs=[HBM],
        out_specs=VMEM,
        scratch_shapes=[pltpu.SemaphoreType.DMA],
        compiler_params=PARAMS,
        cost_estimate=pl.CostEstimate(flops=0, bytes_accessed=2 * MIB, transcendentals=0),
    )(fields)


def far_branch(plane):
    def send(piece):
        return move(piece, shift_pattern(3, [plane])), move(piece, shift_pattern(-3, [plane]))

    return send


def far(piece, plane, distance):
    up, down = lax.switch(plane, [far_branch(p) for p in range(RING)], piece)
    return pick(distance == 3, up, pick(distance == 5, down, piece))


def near_moves(held):
    return move(held, shift_pattern(1)), move(held, shift_pattern(-1))


def near_pick(held, plus, minus, distance):
    keep = (distance == 0) | (distance == 3) | (distance == 5)
    from_low = (distance == 1) | (distance == 4) | (distance == 6)
    return pick(keep, held, pick(from_low, plus, minus))


def ordered(flag, own, got):
    return jnp.stack([pick(flag, got, own), pick(flag, own, got)])


def on_device(perturbations, trajectory, slot_table, step_indices):
    my_z, my_x, my_c = (lax.axis_index(axis) for axis in GROUP_AXES)
    space = lax.axis_index("space")
    on = jnp.stack([space > 0, space < SPACE - 1]).astype(jnp.float32)

    mine, sent, bottom, top, packed = decode_slice(
        trajectory, slot_table, step_indices, perturbations
    )
    other = move(sent, C_PATTERN)
    packed = packed[0]
    owners = [packed % GROUP, packed // GROUP]
    planes = [owner // 4 for owner in owners]
    distance = [(my_z - z) % RING for z in planes]
    low = lax.ppermute(top, "space", FORWARD)
    high = lax.ppermute(bottom, "space", BACKWARD)

    fields = perturbations[0]
    waiting = []
    for owner in owners:
        half = pick(owner % 2 == my_c, mine, other)
        keep = lax.dynamic_index_in_dim(half, my_x, 0, keepdims=False)
        got = move(lax.dynamic_index_in_dim(half, 1 - my_x, 0, keepdims=False), X_PATTERN)
        waiting.append((keep, got))
    pieces = [
        pick((owner // 2) % 2 == my_x, keep, got) for owner, (keep, got) in zip(owners, waiting)
    ]

    first = far(pieces[0], planes[0], distance[0])
    first_moves = near_moves(first)
    second, low, high = lax.optimization_barrier((pieces[1], low, high))
    second = far(second, planes[1], distance[1])
    second, first_moves = lax.optimization_barrier((second, first_moves))
    first = near_pick(first, *first_moves, distance[0])
    pair = ordered(my_x == 1, first, move(first, X_PATTERN))
    second = near_pick(second, *near_moves(second), distance[1])
    got, other = move(second, X_PATTERN), move(pair, C_PATTERN)
    pair, source = lax.optimization_barrier((pair, fields))
    other, fields = lax.optimization_barrier((other, load(source)))
    whole = ordered(my_c == 1, pair, other).reshape(PLANES, 6, LEVELS, WIDTH)
    outer, narrow = first_outer_step(on, fields, high, low, whole)
    got, _ = lax.optimization_barrier((got, narrow))
    low = lax.ppermute(narrow[1], "space", FORWARD)
    high = lax.ppermute(narrow[0], "space", BACKWARD)
    inner = first_inner_step(fields, whole)
    pair = ordered(my_x == 1, second, got)
    whole = lax.all_gather(pair, "c").reshape(PLANES, 6, LEVELS, WIDTH)
    part = second_inner_step(outer, inner, whole)
    part, high, low = lax.optimization_barrier((part, high, low))
    return second_outer_step(on, outer, inner, high, low, whole, part)[None]


def solution(mesh):
    fine = Mesh(mesh.devices.reshape(SPACE, RING, 2, 2), ("space",) + GROUP_AXES)
    return jax.shard_map(
        on_device,
        mesh=fine,
        in_specs=(
            P(GROUP_AXES, None, "space", None, None),
            P(GROUP_AXES, None, "space", None, None),
            P(),
            P(),
        ),
        out_specs=P(GROUP_AXES, None, "space", None, None),
        check_vma=False,
    )
```

```python
import jax
import jax.numpy as jnp
from jax import lax
from jax.experimental import pallas as pl
from jax.experimental.pallas import tpu as pltpu
from jax.sharding import Mesh
from jax.sharding import PartitionSpec as P

STEPS = 2

SATURATION_SLOPE = 2.0
SHARPNESS = 4.0
CONDENSE_RATE = 0.25
LATENT_HEAT = 0.3

GROUP = 32
RING = 8
SPACE = 8
GROUP_AXES = ("z", "x", "c")
PLANES, LEVELS, WIDTH = 4, 64, 256
BLOCK = 16
MIB = 1024 * 1024

VMEM = pl.BlockSpec(memory_space=pltpu.VMEM)
SMEM = pl.BlockSpec(memory_space=pltpu.SMEM)
HBM = pl.BlockSpec(memory_space=pltpu.HBM)


def spot(z, x, c):
    return (z % RING) * 4 + x * 2 + c


def shift_pattern(step, planes=range(RING)):
    return [
        (spot(z, x, c), spot(z + step, x, c)) for z in planes for x in range(2) for c in range(2)
    ]


X_PATTERN = [(i, i ^ 2) for i in range(GROUP)]
C_PATTERN = [(i, i ^ 1) for i in range(GROUP)]
FORWARD = [(i, (i + 1) % SPACE) for i in range(SPACE)]
BACKWARD = [(target, source) for source, target in FORWARD]


def move(value, pattern):
    return lax.ppermute(value, GROUP_AXES, pattern)


def pick(flag, yes, no):
    return jnp.where(flag, yes, no)


def decode_kernel(
    stored_hbm, fields_hbm, keep_ref, send_ref, bottom_ref, top_ref, stored_ref, edge_ref, sems
):
    copies = [
        pltpu.make_async_copy(stored_hbm.at[0, :, p], stored_ref.at[p], sems.at[p])
        for p in range(PLANES)
    ]
    sides = [
        pltpu.make_async_copy(fields_hbm.at[0, :, 3 * k], edge_ref.at[k], sems.at[4 + k])
        for k in range(2)
    ]
    for copy in copies + sides:
        copy.start()
    mine = lax.axis_index("c")
    for p in range(PLANES):
        copies[p].wait()
        values = []
        for start in range(0, LEVELS, 32):
            rows = slice(start, start + 32)
            potential, exner_value, moisture, density = (
                1.0 + scale * stored_ref[p, k, rows, :].astype(jnp.float32)
                for k, scale in ((4, 0.4), (5, 0.4), (6, 2.0), (7, 0.8))
            )
            saturated = jnp.exp(SATURATION_SLOPE * (potential * exner_value - 1.0)) / density
            weight = jax.nn.sigmoid(SHARPNESS * (moisture - saturated))
            uptake = weight.astype(jnp.bfloat16)
            coupling = (weight * SATURATION_SLOPE * exner_value * saturated).astype(jnp.bfloat16)
            stored_ref[p, 4, rows, :] = uptake
            stored_ref[p, 5, rows, :] = coupling

        @pl.when(mine == p // 2)
        def _():
            keep_ref[p % 2] = stored_ref[p, 0:6]

        @pl.when(mine != p // 2)
        def _():
            send_ref[p % 2] = stored_ref[p, 0:6]

    for k, target in enumerate((bottom_ref, top_ref)):
        sides[k].wait()
        target[...] = edge_ref[k].astype(jnp.bfloat16)


def owner_kernel(table_ref, steps_ref, owner_ref):
    owner_ref[0] = table_ref[steps_ref[0]] + GROUP * table_ref[steps_ref[1]]


def packed_owners(slot_table, step_indices):
    return pl.pallas_call(
        owner_kernel,
        out_shape=jax.ShapeDtypeStruct((1,), jnp.int32),
        in_specs=[SMEM] * 2,
        out_specs=SMEM,
    )(slot_table, step_indices)


def decode_slice(trajectory, perturbations):
    half = jax.ShapeDtypeStruct((2, 6, LEVELS, WIDTH), jnp.bfloat16)
    edge = jax.ShapeDtypeStruct((4, LEVELS, WIDTH), jnp.bfloat16)
    return pl.pallas_call(
        decode_kernel,
        out_shape=(half, half, edge, edge),
        in_specs=[HBM] * 2,
        out_specs=(VMEM, VMEM, VMEM, VMEM),
        scratch_shapes=[
            pltpu.VMEM((PLANES, 8, LEVELS, WIDTH), jnp.bfloat16),
            pltpu.VMEM((2, 4, LEVELS, WIDTH), jnp.float32),
            pltpu.SemaphoreType.DMA((6,)),
        ],
        compiler_params=pltpu.CompilerParams(vmem_limit_bytes=52 * MIB),
        cost_estimate=pl.CostEstimate(
            flops=1_500_000, bytes_accessed=3_500_000, transcendentals=200_000
        ),
    )(trajectory, perturbations)


def stencil(coef, centre, west, east, out, west_on=None, east_on=None):
    column = lax.broadcasted_iota(jnp.int32, (BLOCK, WIDTH), 1)
    row = lax.broadcasted_iota(jnp.int32, (BLOCK, WIDTH), 0)
    for start in range(0, LEVELS, BLOCK):
        rows = slice(start, start + BLOCK)
        speed = [coef(k, rows).astype(jnp.float32) for k in range(6)]
        diffusion = 0.025 + 0.06 * speed[3]
        west_w = jnp.maximum(speed[0], 0.0) + diffusion
        east_w = diffusion - jnp.minimum(speed[0], 0.0)
        south_w = jnp.maximum(speed[1], 0.0) + diffusion
        north_w = diffusion - jnp.minimum(speed[1], 0.0)
        below_w = jnp.maximum(speed[2], 0.0) + diffusion
        above_w = diffusion - jnp.minimum(speed[2], 0.0)
        centre_w = 1.0 - (west_w + east_w + south_w + north_w + below_w + above_w)
        south_w = jnp.where(column == 0, 0.0, south_w)
        north_w = jnp.where(column == WIDTH - 1, 0.0, north_w)
        if start == 0:
            below_w = jnp.where(row == 0, 0.0, below_w)
        if start + BLOCK == LEVELS:
            above_w = jnp.where(row == BLOCK - 1, 0.0, above_w)
        if west_on is not None:
            west_w = west_w * west_on
        if east_on is not None:
            east_w = east_w * east_on
        carried = []
        for field in range(4):
            here = centre(field, rows)
            if start == 0:
                below = pltpu.roll(here, 1, 0)
            else:
                below = centre(field, slice(start - 1, start + BLOCK - 1))
            if start + BLOCK == LEVELS:
                above = pltpu.roll(here, BLOCK - 1, 0)
            else:
                above = centre(field, slice(start + 1, start + BLOCK + 1))
            carried.append(
                (centre_w * here + west_w * west(field, rows))
                + (east_w * east(field, rows) + south_w * pltpu.roll(here, 1, 1))
                + (north_w * pltpu.roll(here, WIDTH - 1, 1) + below_w * below)
                + above_w * above
            )
        condense = CONDENSE_RATE * (speed[4] * carried[1] - speed[5] * carried[0])
        out(0, rows, carried[0] + LATENT_HEAT * condense)
        out(1, rows, carried[1] - condense)
        out(2, rows, carried[2] + condense)
        out(3, rows, carried[3])


def reader(ref, plane):
    return lambda field, rows: ref[field, plane, rows, :].astype(jnp.float32)


def writer(ref, plane):
    def write(field, rows, value):
        ref[field, plane, rows, :] = value

    return write


def coefficient(ref, plane):
    return lambda k, rows: ref[plane, k, rows, :]


def edge_reader(ref):
    return lambda field, rows: ref[field, rows, :].astype(jnp.float32)


def pair_reader(ref, k):
    return lambda field, rows: ref[k, field, rows, :].astype(jnp.float32)


def both_writer(ref, narrow_ref, k):
    def write(field, rows, value):
        ref[k, field, rows, :] = value
        narrow_ref[k, field, rows, :] = value.astype(jnp.bfloat16)

    return write


def pair_writer(ref, k):
    def write(field, rows, value):
        ref[k, field, rows, :] = value

    return write


def first_outer(on_ref, q_ref, high_ref, low_ref, coef_ref, out_ref, narrow_ref):
    stencil(
        coefficient(coef_ref, 0), reader(q_ref, 0), edge_reader(low_ref), reader(q_ref, 1),
        both_writer(out_ref, narrow_ref, 0), west_on=on_ref[0],
    )
    stencil(
        coefficient(coef_ref, 3), reader(q_ref, 3), reader(q_ref, 2), edge_reader(high_ref),
        both_writer(out_ref, narrow_ref, 1), east_on=on_ref[1],
    )


def first_inner(q_ref, coef_ref, out_ref):
    for p in (1, 2):
        stencil(
            coefficient(coef_ref, p), reader(q_ref, p), reader(q_ref, p - 1), reader(q_ref, p + 1),
            pair_writer(out_ref, p - 1),
        )


def second_inner(outer_ref, inner_ref, coef_ref, out_hbm, out_ref, sems):
    planes = [pair_reader(outer_ref, 0), pair_reader(inner_ref, 0), pair_reader(inner_ref, 1), pair_reader(outer_ref, 1)]
    copies = []
    for p in (1, 2):
        stencil(
            coefficient(coef_ref, p), planes[p], planes[p - 1], planes[p + 1],
            pair_writer(out_ref, p - 1),
        )
        copies.append(pltpu.make_async_copy(out_ref.at[p - 1], out_hbm.at[:, p], sems.at[p - 1]))
        copies[-1].start()
    for copy in copies:
        copy.wait()


def second_outer(
    on_ref, outer_ref, inner_ref, high_ref, low_ref, coef_ref, part_hbm, out_hbm, out_ref, sems
):
    stencil(
        coefficient(coef_ref, 0), pair_reader(outer_ref, 0), edge_reader(low_ref),
        pair_reader(inner_ref, 0), pair_writer(out_ref, 0), west_on=on_ref[0],
    )
    low_copy = pltpu.make_async_copy(out_ref.at[0], out_hbm.at[:, 0], sems.at[0])
    low_copy.start()
    stencil(
        coefficient(coef_ref, 3), pair_reader(outer_ref, 1), pair_reader(inner_ref, 1),
        edge_reader(high_ref), pair_writer(out_ref, 1), east_on=on_ref[1],
    )
    high_copy = pltpu.make_async_copy(out_ref.at[1], out_hbm.at[:, 3], sems.at[1])
    high_copy.start()
    low_copy.wait()
    high_copy.wait()


PAIR = (2, 4, LEVELS, WIDTH)
WHOLE = jax.ShapeDtypeStruct((4, PLANES, LEVELS, WIDTH), jnp.float32)
COST = pl.CostEstimate(flops=4_000_000, bytes_accessed=3_000_000, transcendentals=0)
PARAMS = pltpu.CompilerParams(vmem_limit_bytes=16 * MIB)


def first_outer_step(*arrays):
    return pl.pallas_call(
        first_outer,
        out_shape=(
            jax.ShapeDtypeStruct(PAIR, jnp.float32),
            jax.ShapeDtypeStruct(PAIR, jnp.bfloat16),
        ),
        in_specs=[SMEM] + [VMEM] * 4,
        out_specs=(VMEM, VMEM),
        compiler_params=PARAMS,
        cost_estimate=COST,
    )(*arrays)


def first_inner_step(*arrays):
    return pl.pallas_call(
        first_inner,
        out_shape=jax.ShapeDtypeStruct(PAIR, jnp.float32),
        in_specs=[VMEM] * 2,
        out_specs=VMEM,
        compiler_params=PARAMS,
        cost_estimate=COST,
    )(*arrays)


def second_inner_step(*arrays):
    return pl.pallas_call(
        second_inner,
        out_shape=WHOLE,
        in_specs=[VMEM] * 3,
        out_specs=HBM,
        scratch_shapes=[pltpu.VMEM(PAIR, jnp.float32), pltpu.SemaphoreType.DMA((2,))],
        compiler_params=PARAMS,
        cost_estimate=COST,
    )(*arrays)


def second_outer_step(*arrays):
    return pl.pallas_call(
        second_outer,
        out_shape=WHOLE,
        in_specs=[SMEM] + [VMEM] * 5 + [HBM],
        out_specs=HBM,
        scratch_shapes=[pltpu.VMEM(PAIR, jnp.float32), pltpu.SemaphoreType.DMA((2,))],
        input_output_aliases={6: 0},
        compiler_params=PARAMS,
        cost_estimate=COST,
    )(*arrays)


def load_kernel(source_hbm, target_ref, sem):
    copy = pltpu.make_async_copy(source_hbm, target_ref, sem)
    copy.start()
    copy.wait()


def load(fields):
    return pl.pallas_call(
        load_kernel,
        out_shape=WHOLE,
        in_specs=[HBM],
        out_specs=VMEM,
        scratch_shapes=[pltpu.SemaphoreType.DMA],
        compiler_params=PARAMS,
        cost_estimate=pl.CostEstimate(flops=0, bytes_accessed=2 * MIB, transcendentals=0),
    )(fields)


def far_branch(plane):
    def send(piece):
        return move(piece, shift_pattern(3, [plane])), move(piece, shift_pattern(-3, [plane]))

    return send


def far(piece, plane, distance):
    up, down = lax.switch(plane, [far_branch(p) for p in range(RING)], piece)
    return pick(distance == 3, up, pick(distance == 5, down, piece))


def near_moves(held):
    return move(held, shift_pattern(1)), move(held, shift_pattern(-1))


def near_pick(held, plus, minus, distance):
    keep = (distance == 0) | (distance == 3) | (distance == 5)
    from_low = (distance == 1) | (distance == 4) | (distance == 6)
    return pick(keep, held, pick(from_low, plus, minus))


def ordered(flag, own, got):
    return jnp.stack([pick(flag, got, own), pick(flag, own, got)])


def on_device(perturbations, trajectory, slot_table, step_indices):
    my_z, my_x, my_c = (lax.axis_index(axis) for axis in GROUP_AXES)
    space = lax.axis_index("space")
    on = jnp.stack([space > 0, space < SPACE - 1]).astype(jnp.float32)

    mine, sent, bottom, top = decode_slice(trajectory, perturbations)
    other = move(sent, C_PATTERN)
    packed = packed_owners(slot_table, step_indices)[0]
    owners = [packed % GROUP, packed // GROUP]
    planes = [owner // 4 for owner in owners]
    distance = [(my_z - z) % RING for z in planes]
    low = lax.ppermute(top, "space", FORWARD)
    high = lax.ppermute(bottom, "space", BACKWARD)

    fields = perturbations[0]
    waiting = []
    for owner in owners:
        half = pick(owner % 2 == my_c, mine, other)
        keep = lax.dynamic_index_in_dim(half, my_x, 0, keepdims=False)
        got = move(lax.dynamic_index_in_dim(half, 1 - my_x, 0, keepdims=False), X_PATTERN)
        waiting.append((keep, got))
    pieces = [
        pick((owner // 2) % 2 == my_x, keep, got) for owner, (keep, got) in zip(owners, waiting)
    ]

    first = far(pieces[0], planes[0], distance[0])
    first_moves = near_moves(first)
    second, low, high = lax.optimization_barrier((pieces[1], low, high))
    second = far(second, planes[1], distance[1])
    second, first_moves = lax.optimization_barrier((second, first_moves))
    first = near_pick(first, *first_moves, distance[0])
    pair = ordered(my_x == 1, first, move(first, X_PATTERN))
    second = near_pick(second, *near_moves(second), distance[1])
    got, other = move(second, X_PATTERN), move(pair, C_PATTERN)
    pair, source = lax.optimization_barrier((pair, fields))
    other, fields = lax.optimization_barrier((other, load(source)))
    whole = ordered(my_c == 1, pair, other).reshape(PLANES, 6, LEVELS, WIDTH)
    outer, narrow = first_outer_step(on, fields, high, low, whole)
    got, _ = lax.optimization_barrier((got, narrow))
    low = lax.ppermute(narrow[1], "space", FORWARD)
    high = lax.ppermute(narrow[0], "space", BACKWARD)
    inner = first_inner_step(fields, whole)
    pair = ordered(my_x == 1, second, got)
    whole = lax.all_gather(pair, "c").reshape(PLANES, 6, LEVELS, WIDTH)
    part = second_inner_step(outer, inner, whole)
    part, high, low = lax.optimization_barrier((part, high, low))
    return second_outer_step(on, outer, inner, high, low, whole, part)[None]


def solution(mesh):
    fine = Mesh(mesh.devices.reshape(SPACE, RING, 2, 2), ("space",) + GROUP_AXES)
    return jax.shard_map(
        on_device,
        mesh=fine,
        in_specs=(
            P(GROUP_AXES, None, "space", None, None),
            P(GROUP_AXES, None, "space", None, None),
            P(),
            P(),
        ),
        out_specs=P(GROUP_AXES, None, "space", None, None),
        check_vma=False,
    )
```
